256 devices in a mesh: row: 8 (over z_lo, core), col: 8 (over x, z_hi), fsdp: 4 (over y).
Axes of the slice: x: 4, y: 4, z: 8 (z_hi: 2, z_lo: 4; z = z_hi * 4 + z_lo), core: 2. Of those that a mesh axis runs over, the one named last changes fastest.
Arguments:
- video: bfloat16 [4, 3, 64, 256, 256], P('fsdp', None, 'row', 'col'), may hold values from -6 to 6
- kernel: bfloat16 [6912, 256], P(None, 'fsdp'), may hold values from -0.078125 to 0.078125
- bias_vec: float32 [256], replicated, may hold values from -3 to 3
- cotangent: bfloat16 [4, 3, 32, 128, 256], P('fsdp', None, 'row', 'col'), may hold values from -6 to 6
Outputs:
- activated: bfloat16 [4, 3, 32, 128, 256], P('fsdp', None, 'row', 'col')
- video_grad: bfloat16 [4, 3, 64, 256, 256], P('fsdp', None, 'row', 'col')
- kernel_grad: float32 [6912, 256], P(('row', 'col'), 'fsdp')
- bias_grad: float32 [256], replicated
The draws below stay inside these ranges and needn't reach their ends.
All inputs are finite; a program needn't handle non-finite values.
Results may differ from the reference program's by a relative error of at most 0.007.
Values may be sent and summed in bfloat16 or wider, within the bound.
A program may use at most 64 MiB of HBM per device.

```python
import math
import jax
import jax.numpy as jnp
from jax import lax

CI = 256
CO = 256
FR = 3
BATCH = 4
HEIGHT = 64
WIDTH = 256
KROWS = 6912
TOKENS = 49152


def with_spikes(values, key, source, target, shards_of, factor):
    owner, partner = [(jnp.arange(values.shape[position]) // (values.shape[position] // shards_of)).reshape([-1 if axis == position else 1 for axis in range(values.ndim)]) for position in (source, target)]
    chosen = jax.random.permutation(key, shards_of)[partner]
    strong = (owner == chosen) | (owner == (partner + shards_of // 2) % shards_of)
    return jnp.where(strong, factor * values, values)


def levels(key, extent, pieces, low, high):
    def one(axis_at, blocks):
        steps = jax.random.uniform(jax.random.fold_in(jax.random.fold_in(key, 6), axis_at), (blocks,), jnp.float32, low / len(pieces), high / len(pieces))
        return jnp.repeat(jnp.exp(steps), extent[axis_at] // blocks).reshape((-1,) + (1,) * (len(extent) - axis_at - 1))

    gain = one(*pieces[0])
    for cut in pieces[1:]:
        gain = gain * one(*cut)
    return gain


def noise(key, dims, spread, reach, split=(), dtype=jnp.bfloat16):
    level = levels(key, dims, split, -0.22, 0.18) if split else 1.0
    drawn = jax.random.normal(key, dims, jnp.float32) * spread * level
    return jnp.minimum(jnp.maximum(drawn, -reach), reach).astype(dtype)


def gaussian_with(stream_key, extent, deviation, reach, split, heavy, kind=jnp.bfloat16):
    drawn = deviation * jax.random.normal(stream_key, extent, jnp.float32)
    if split:
        drawn = drawn * levels(stream_key, extent, split, -0.22, 0.18)
    return jnp.clip(with_spikes(drawn, jax.random.fold_in(stream_key, 3), *heavy), -reach, reach).astype(kind)


def setup_inputs(seed: int = 0) -> dict:
    seeds = jax.random.split(jax.random.key(seed), 5)
    video = gaussian_with(seeds[0], (BATCH, FR, HEIGHT, WIDTH, CI), 1.0, 6.0, ((0, 4), (2, 8), (3, 8)), (3, 4, 8, 2.0))
    kernel = noise(seeds[1], (KROWS, CO), KROWS ** -0.5, 0.078125, ((1, 4),))
    bias_vec = noise(seeds[2], (CO,), 0.5, 3.0, (), jnp.float32)
    cotangent = gaussian_with(seeds[3], (BATCH, FR, HEIGHT // 2, WIDTH // 2, CO), 1.0, 6.0, ((0, 4), (2, 8), (3, 8)), (2, 4, 8, 2.0))
    return {"video": video, "kernel": kernel, "bias_vec": bias_vec, "cotangent": cotangent}


def reference(video, kernel, bias_vec, cotangent):
    video_f = video.astype(jnp.float32)
    kernel_f = kernel.astype(jnp.float32).reshape(3, 3, 3, CI, CO)

    def convolve(clips, weights):
        padded = jnp.concatenate([clips[:, :1], clips[:, :1], clips], axis=1)
        return lax.conv_general_dilated(padded, weights, (1, 2, 2), ((0, 0), (1, 0), (1, 0)), dimension_numbers=('NDHWC', 'DHWIO', 'NDHWC'), precision=lax.Precision.HIGHEST)
    linear, pullback = jax.vjp(convolve, video_f, kernel_f)
    preact = linear + bias_vec.astype(jnp.float32)
    sigma = jax.nn.sigmoid(preact)
    activated = (preact * sigma).astype(jnp.bfloat16)
    slope = cotangent.astype(jnp.float32) * sigma * (1.0 + preact * (1.0 - sigma))
    delta = lax.optimization_barrier(slope.astype(jnp.bfloat16)).astype(jnp.float32)
    video_grad, kernel_grad = pullback(delta)
    factor = 1.0 / math.sqrt(TOKENS)
    return (activated, video_grad.astype(jnp.bfloat16), kernel_grad.reshape(KROWS, CO) * factor, lax.optimization_barrier(jnp.sum(delta, axis=(0, 1, 2, 3))) * factor)
```

```python
import math

import jax
import jax.numpy as jnp
from jax import lax
from jax.experimental import pallas as pl
from jax.experimental.pallas import tpu as pltpu
from jax.sharding import PartitionSpec as P

MESH = pl.DeviceIdType.MESH
F32 = jnp.float32
BF16 = jnp.bfloat16

TAPS = 27
CI = 256
CO = 256
SHARD = 64
KROWS = TAPS * CI
TOK = 192
PITCH = 40
VIA_X = 896
ROUND = 4 * VIA_X
DIRECT = KROWS - ROUND
BLOCK = 864
WINDOW = 224
PIECE = 108
FACTOR = 1.0 / math.sqrt(49152)


def frame_of(t, p):
    return max(t + p - 2, 0)


def nt(a, b):
    return lax.dot_general(a, b, (((1,), (1,)), ((), ())), preferred_element_type=F32)


def nn(a, b):
    return jnp.dot(a, b, preferred_element_type=F32)


def identity(n):
    rows = lax.broadcasted_iota(jnp.int32, (n, n), 0)
    cols = lax.broadcasted_iota(jnp.int32, (n, n), 1)
    return (rows == cols).astype(F32).astype(BF16)


PLANE = 27 * PITCH


def take(flat, start, count, stride):
    return jnp.concatenate(
        [flat[pl.ds(n * PLANE + start, count, stride=stride), :] for n in range(2)], axis=1
    )


def put(flat, start, count, stride, value):
    for n in range(2):
        flat[pl.ds(n * PLANE + start, count, stride=stride), :] = value[:, 128 * n : 128 * n + 128]


def swap_halves(value):
    return jnp.concatenate(
        [pltpu.roll(value[:, 128 * n : 128 * n + 128], 64, 1) for n in range(value.shape[1] // 128)],
        axis=1,
    )


def kernel_body(
    video,
    kernel,
    bias,
    cot,
    act_out,
    vg_out,
    kg_out,
    bg_out,
    kin,
    kt,
    vid,
    cotv,
    vpad,
    hl_send,
    hc_send,
    hl,
    hu,
    hc,
    patches,
    pt,
    pts,
    dl,
    dlx,
    dls,
    dlsx,
    w,
    ra,
    rb,
    sa,
    sb,
    ra2,
    rb2,
    tt,
    zz,
    rz,
    by,
    bx,
    bz,
    g,
    gl_send,
    gc_send,
    gu,
    gl,
    gc,
    lsem,
    k_s,
    k_r,
    h_s,
    h_r,
    c_s,
    c_r,
    r1_s,
    r1_r,
    r2_s,
    r2_r,
    r3_s,
    r3_r,
    b_s,
    b_r,
):
    row = lax.axis_index("row")
    col = lax.axis_index("col")
    y = lax.axis_index("fsdp")
    core = lax.rem(row, 2)
    zl = row // 2
    x = col // 2
    zh = lax.rem(col, 2)
    z = zh * 4 + zl

    def to_y(n):
        return {"row": row, "col": col, "fsdp": lax.rem(y + n, 4)}

    def to_x(n):
        return {"row": row, "col": lax.rem(x + n, 4) * 2 + zh, "fsdp": y}

    def to_z(n):
        there = lax.rem(z + n, 8)
        return {
            "row": lax.rem(there, 4) * 2 + core,
            "col": x * 2 + there // 4,
            "fsdp": y,
        }

    def to_tile(rows, cols):
        return {"row": lax.rem(row + rows + 8, 8), "col": lax.rem(col + cols + 8, 8), "fsdp": y}

    sibling = {"row": row + 1 - 2 * core, "col": col, "fsdp": y}

    def remote(src, dst, ss, rs, where):
        return pltpu.make_async_remote_copy(
            src_ref=src, dst_ref=dst, send_sem=ss, recv_sem=rs, device_id=where, device_id_type=MESH
        )

    load_k = pltpu.make_async_copy(kernel, kin, lsem.at[0])
    load_v = pltpu.make_async_copy(video.at[0], vid, lsem.at[1])
    load_c = pltpu.make_async_copy(cot.at[0], cotv, lsem.at[2])
    load_k.start()
    load_v.start()
    load_c.start()

    partners = [to_y(n) for n in (1, 2, 3)] + [to_x(n) for n in (1, 2, 3)]
    partners += [to_z(n) for n in range(1, 8)] + [sibling]
    partners += [to_tile(a, b) for a, b in ((0, 1), (0, -1), (1, 0), (-1, 0), (1, 1), (-1, -1))]
    barrier = pltpu.get_barrier_semaphore()
    for partner in partners:
        pl.semaphore_signal(barrier, inc=1, device_id=partner, device_id_type=MESH)

    own_rows = pl.multiple_of(y * SHARD, SHARD)
    load_k.wait()
    kt[pl.ds(own_rows, SHARD), :] = nt(identity(SHARD), kin[...]).astype(BF16)
    load_v.wait()
    for f in range(3):
        for r in range(8):
            for n in range(2):
                vpad[n, (r + 1) * 3 + f, 8:40, :] = vid[f, r, :, 128 * n : 128 * n + 128].astype(F32)
    flat = vpad.reshape(2 * PLANE, 128)
    hl_send[...] = take(flat, 3 * PITCH + 39, 24, PITCH)
    hc_send[0:3, :] = hl_send[21:24, :]

    pl.semaphore_wait(barrier, len(partners))

    half_rows = pl.multiple_of(y * SHARD + core * 32, 32)
    via = pl.multiple_of(x * VIA_X, 128)

    def shard_rows(n):
        return pl.multiple_of(lax.rem(y + n, 4) * SHARD + core * 32, 32)

    def other_rows(n):
        return pl.multiple_of(lax.rem(y + n, 4) * SHARD + (1 - core) * 32, 32)

    first = []
    for n in (1, 3, 2):
        ref = kt.at[pl.ds(half_rows, 32), pl.ds(via, VIA_X)]
        first.append(remote(ref, ref, k_s.at[n - 1], k_r.at[n - 1], to_y(n)))
        first[-1].start()
    halos = [
        remote(hl_send, hl, h_s.at[0], h_r.at[0], to_tile(0, 1)),
        remote(vid.at[:, 7], hu, h_s.at[1], h_r.at[1], to_tile(1, 0)),
        remote(hc_send, hc, h_s.at[2], h_r.at[2], to_tile(1, 1)),
    ]
    for copy in halos:
        copy.start()
    direct = []
    for n in (1, 3, 2):
        ref = kt.at[pl.ds(half_rows, 32), pl.ds(ROUND, DIRECT)]
        direct.append(remote(ref, ref, k_s.at[2 + n], k_r.at[2 + n], to_y(n)))
        direct[-1].start()

    relayed = []
    for at, n in enumerate((1, 3, 2)):
        first[at].wait_recv()
        rows = shard_rows(4 - n)
        ref = kt.at[pl.ds(rows, 32), pl.ds(via, VIA_X)]
        for m in (1, 3, 2):
            slot = 6 + (n - 1) * 3 + m - 1
            relayed.append(remote(ref, ref, k_s.at[slot], k_r.at[slot], to_x(m)))
            relayed[-1].start()

    for copy in halos:
        copy.wait_recv()
    for f in range(3):
        top = hu[f].astype(F32)
        top = jnp.where(row > 0, top, 0.0)
        for n in range(2):
            vpad[n, f, 8:40, :] = top[:, 128 * n : 128 * n + 128]
    put(flat, 3 * PITCH + 7, 24, PITCH, jnp.where(col > 0, hl[...], 0.0))
    corner = jnp.where((row > 0) & (col > 0), hc[...], 0.0)
    for f in range(3):
        for n in range(2):
            vpad[n, f, 7:8, :] = corner[f : f + 1, 128 * n : 128 * n + 128]
    for r in range(9):
        for f in range(3):
            for s in range(3):
                block = take(flat, (r * 3 + f) * PITCH + 7 + s, 16, 2).astype(BF16)
                for t in range(3):
                    for p in range(3):
                        if frame_of(t, p) != f:
                            continue
                        for q in range(3):
                            i, odd = divmod(r - q, 2)
                            if odd or not 0 <= i < 4:
                                continue
                            tap = (p * 3 + q) * 3 + s
                            patches[
                                (t * 4 + i) * 16 : (t * 4 + i) * 16 + 16, tap * CI : tap * CI + CI
                            ] = block
    unit = identity(CI)
    for tap in range(TAPS):
        pt[tap * CI : tap * CI + CI, :] = nt(unit, patches[:, tap * CI : tap * CI + CI]).astype(BF16)
    swaps = []
    for n in range(4):
        base = pl.multiple_of(n * 2 * BLOCK + (1 - core) * BLOCK, 32)
        swaps.append(remote(pt.at[pl.ds(base, BLOCK), :], pts.at[n], c_s.at[n], c_r.at[n], sibling))
        swaps[-1].start()

    passed = []
    for at, n in enumerate((1, 3, 2)):
        direct[at].wait_recv()
        ref = kt.at[pl.ds(shard_rows(4 - n), 32), pl.ds(ROUND, DIRECT)]
        passed.append(remote(ref, ref, c_s.at[3 + n], c_r.at[3 + n], sibling))
        passed[-1].start()
    for at, n in enumerate((1, 3, 2)):
        for m in range(3):
            relayed[at * 3 + m].wait_recv()
        ref = kt.at[pl.ds(shard_rows(4 - n), 32), pl.ds(0, ROUND)]
        passed.append(remote(ref, ref, c_s.at[6 + n], c_r.at[6 + n], sibling))
        passed[-1].start()
    for copy in passed:
        copy.wait_recv()

    preact = nt(patches[...], kt[...]) + bias[...]
    sigma = jax.nn.sigmoid(preact)
    act_out[...] = (preact * sigma).astype(BF16).reshape(1, 3, 4, 16, CO)
    load_c.wait()
    slope = cotv[...].reshape(TOK, CO).astype(F32) * sigma * (1.0 + preact * (1.0 - sigma))
    delta = slope.astype(BF16)
    dl[...] = delta
    swap_delta = remote(dl, dls, c_s.at[10], c_r.at[10], sibling)
    swap_delta.start()
    delta_f = delta.astype(F32)
    dlx[...] = swap_halves(delta_f).astype(BF16)
    bias_own = jnp.sum(delta_f, axis=0, keepdims=True)

    swap_delta.wait_recv()
    delta_s = dls[...].astype(F32)
    dlsx[...] = swap_halves(delta_s).astype(BF16)
    bias_chip = bias_own + jnp.sum(delta_s, axis=0, keepdims=True)
    by[y] = jnp.broadcast_to(bias_chip, (8, CO))
    for copy in swaps:
        copy.wait_recv()

    low = lax.broadcasted_iota(jnp.int32, (144, 128), 1) < 64
    phase1 = []
    for part in range(2):
        for step in range(6):
            lo_at = pl.multiple_of(part * 2 * BLOCK + core * BLOCK + step * 144, 16)
            hi_at = pl.multiple_of((part + 2) * 2 * BLOCK + core * BLOCK + step * 144, 16)
            here = slice(step * 144, step * 144 + 144)
            lo = nn(pt[pl.ds(lo_at, 144), :], dl[...]) + nn(pts[part, here, :], dls[...])
            hi = nn(pt[pl.ds(hi_at, 144), :], dlx[...]) + nn(pts[part + 2, here, :], dlsx[...])
            for n in range(4):
                cols = slice(128 * (n // 2), 128 * (n // 2) + 128)
                if n % 2:
                    w[part, n, here, :] = jnp.where(low, hi[:, cols], lo[:, cols]).astype(BF16)
                else:
                    w[part, n, here, :] = jnp.where(low, lo[:, cols], hi[:, cols]).astype(BF16)
        for n in (1, 3, 2):
            if part == 0:
                phase1.append(
                    remote(w.at[0, lax.rem(y + n, 4)], ra.at[n - 1], r1_s.at[n - 1], r1_r.at[n - 1], to_y(n))
                )
            else:
                start = pl.multiple_of(16 * (27 * lax.rem(x + n, 4) // 2), 16)
                phase1.append(
                    remote(
                        w.at[1, :, pl.ds(start, WINDOW), :],
                        rb.at[n - 1],
                        r1_s.at[2 + n],
                        r1_r.at[2 + n],
                        to_x(n),
                    )
                )
            phase1[-1].start()
        if part == 0:
            bias_y = [remote(by.at[y], by.at[y], b_s.at[n - 1], b_r.at[n - 1], to_y(n)) for n in (1, 2, 3)]
            for copy in bias_y:
                copy.start()

    g[...] = jnp.zeros_like(g)
    gflat = g.reshape(2 * PLANE, 128)
    for q in range(3):
        for s in range(3):
            d = [
                nn(dl[...], kt[:, ((p * 3 + q) * 3 + s) * CI : ((p * 3 + q) * 3 + s) * CI + CI])
                for p in range(3)
            ]
            frames = [
                d[0][0:64] + d[0][64:128] + d[0][128:192] + d[1][0:64] + d[1][64:128] + d[2][0:64],
                d[1][128:192] + d[2][64:128],
                d[2][128:192],
            ]
            for f in range(3):
                for i in range(4):
                    at = ((q + 2 * i) * 3 + f) * PITCH + 7 + s
                    sofar = take(gflat, at, 16, 2)
                    put(gflat, at, 16, 2, sofar + frames[f][16 * i : 16 * i + 16])
    gl_send[...] = take(gflat, 3 * PITCH + 7, 24, PITCH)
    for f in range(3):
        for n in range(2):
            gc_send[f : f + 1, 128 * n : 128 * n + 128] = g[n, f, 7:8, :]
    edges = [
        remote(gl_send, gl, h_s.at[3], h_r.at[3], to_tile(0, -1)),
        remote(g.at[:, pl.ds(0, 3), pl.ds(8, 32), :], gu, h_s.at[4], h_r.at[4], to_tile(-1, 0)),
        remote(gc_send, gc, h_s.at[5], h_r.at[5], to_tile(-1, -1)),
    ]
    for copy in edges:
        copy.start()

    for copy in bias_y:
        copy.wait_recv()
    bx[x] = by[0] + by[1] + by[2] + by[3]
    bias_x = [remote(bx.at[x], bx.at[x], b_s.at[2 + n], b_r.at[2 + n], to_x(n)) for n in (1, 2, 3)]
    for copy in bias_x:
        copy.start()

    for copy in phase1[:3]:
        copy.wait_recv()
    sa[...] = (
        w[0, y].astype(F32) + ra[0].astype(F32) + ra[1].astype(F32) + ra[2].astype(F32)
    ).astype(BF16)
    phase2 = []
    for n in (1, 3, 2):
        start = pl.multiple_of(16 * (27 * lax.rem(x + n, 4) // 2), 16)
        phase2.append(
            remote(sa.at[pl.ds(start, WINDOW), :], ra2.at[n - 1], r2_s.at[n - 1], r2_r.at[n - 1], to_x(n))
        )
        phase2[-1].start()
    own = pl.multiple_of(16 * (27 * x // 2), 16)
    for copy in phase1[3:]:
        copy.wait_recv()
    sb[...] = (
        w[1, :, pl.ds(own, WINDOW), :].astype(F32)
        + rb[0].astype(F32)
        + rb[1].astype(F32)
        + rb[2].astype(F32)
    ).astype(BF16)
    for n in (1, 3, 2):
        phase2.append(
            remote(sb.at[lax.rem(y + n, 4)], rb2.at[n - 1], r2_s.at[2 + n], r2_r.at[2 + n], to_y(n))
        )
        phase2[-1].start()

    for copy in edges:
        copy.wait_recv()
    for f in range(3):
        for n in range(2):
            g[n, 24 + f, 8:40, :] += jnp.where(row < 7, gu[n, f], 0.0)
    sofar = take(gflat, 3 * PITCH + 39, 24, PITCH)
    put(gflat, 3 * PITCH + 39, 24, PITCH, sofar + jnp.where(col < 7, gl[...], 0.0))
    corner = jnp.where((row < 7) & (col < 7), gc[...], 0.0)
    for f in range(3):
        for n in range(2):
            g[n, 24 + f, 39:40, :] += corner[f : f + 1, 128 * n : 128 * n + 128]
    for f in range(3):
        for r in range(8):
            for n in range(2):
                vg_out[0, f, r, :, 128 * n : 128 * n + 128] = g[n, (r + 1) * 3 + f, 8:40, :].astype(BF16)

    for copy in bias_x:
        copy.wait_recv()
    bz[z] = bx[0] + bx[1] + bx[2] + bx[3]
    bias_z = [remote(bz.at[z], bz.at[z], b_s.at[5 + n], b_r.at[5 + n], to_z(n)) for n in range(1, 8)]
    for copy in bias_z:
        copy.start()

    odd = lax.rem(y, 2) == 1
    offset = 8 * lax.rem(x, 2)
    first_half = lax.broadcasted_iota(jnp.int32, (64, 128), 1) < 64
    tt[:, WINDOW:, :] = jnp.zeros((2, 24, 128), F32)
    for part in range(2):
        for copy in phase2[3 * part : 3 * part + 3]:
            copy.wait_recv()
        if part == 0:
            total = sa[pl.ds(own, WINDOW), :].astype(F32)
            for n in range(3):
                total = total + ra2[n].astype(F32)
        else:
            total = sb[y].astype(F32)
            for n in range(3):
                total = total + rb2[n].astype(F32)
        tt[part, 0:WINDOW, :] = jnp.where(odd, pltpu.roll(total, 64, 1), total)
        for half in range(2):
            u = tt[part, pl.ds(offset + PIECE * half, 128), :]
            a, b = u[0:64], u[64:128]
            zz[half * 4 + part] = jnp.where(first_half, a, pltpu.roll(b, 64, 1)).astype(BF16)
            zz[half * 4 + 2 + part] = jnp.where(first_half, pltpu.roll(a, 64, 1), b).astype(BF16)
    phase3 = []
    for n in (4, 3, 5, 2, 6, 1, 7):
        phase3.append(
            remote(zz.at[lax.rem(z + n, 8)], rz.at[n - 1], r3_s.at[n - 1], r3_r.at[n - 1], to_z(n))
        )
        phase3[-1].start()

    for copy in bias_z:
        copy.wait_recv()
    total = bz[0]
    for n in range(1, 8):
        total = total + bz[n]
    bg_out[...] = total[0:1] * FACTOR

    for copy in phase3:
        copy.wait_recv()
    total = zz[z].astype(F32)
    for n in range(7):
        total = total + rz[n].astype(F32)
    total = total * FACTOR
    kg_out[0:64, :] = total[:, 0:64]
    kg_out[64:PIECE, :] = pltpu.roll(total, 64, 1)[0 : PIECE - 64, 0:64]

    for copies in (
        first, halos, direct, relayed, swaps, passed, [swap_delta], phase1, bias_y, edges, bias_x,
        phase2, bias_z, phase3,
    ):
        for copy in copies:
            copy.wait_send()


def body(video, kernel, bias_vec, cotangent):
    dma = pltpu.SemaphoreType.DMA
    vmem = pltpu.VMEM
    activated, video_grad, kernel_grad, bias_grad = pl.pallas_call(
        kernel_body,
        out_shape=(
            jax.ShapeDtypeStruct((1, 3, 4, 16, CO), BF16),
            jax.ShapeDtypeStruct((1, 3, 8, 32, CI), BF16),
            jax.ShapeDtypeStruct((PIECE, SHARD), F32),
            jax.ShapeDtypeStruct((1, CO), F32),
        ),
        in_specs=[
            pl.BlockSpec(memory_space=pl.ANY),
            pl.BlockSpec(memory_space=pl.ANY),
            pl.BlockSpec(memory_space=pltpu.VMEM),
            pl.BlockSpec(memory_space=pl.ANY),
        ],
        out_specs=tuple(pl.BlockSpec(memory_space=pltpu.VMEM) for _ in range(4)),
        scratch_shapes=[
            vmem((KROWS, SHARD), BF16),
            vmem((CO, KROWS), BF16),
            vmem((3, 8, 32, CI), BF16),
            vmem((3, 4, 16, CO), BF16),
            vmem((2, 27, PITCH, 128), F32),
            vmem((24, CI), F32),
            vmem((8, CI), F32),
            vmem((24, CI), F32),
            vmem((3, 32, CI), BF16),
            vmem((8, CI), F32),
            vmem((TOK, KROWS), BF16),
            vmem((KROWS, TOK), BF16),
            vmem((4, BLOCK, TOK), BF16),
            vmem((TOK, CO), BF16),
            vmem((TOK, CO), BF16),
            vmem((TOK, CO), BF16),
            vmem((TOK, CO), BF16),
            vmem((2, 4, BLOCK, 128), BF16),
            vmem((3, BLOCK, 128), BF16),
            vmem((3, 4, WINDOW, 128), BF16),
            vmem((BLOCK, 128), BF16),
            vmem((4, WINDOW, 128), BF16),
            vmem((3, WINDOW, 128), BF16),
            vmem((3, WINDOW, 128), BF16),
            vmem((2, WINDOW + 24, 128), F32),
            vmem((8, 64, 128), BF16),
            vmem((7, 64, 128), BF16),
            vmem((4, 8, CO), F32),
            vmem((4, 8, CO), F32),
            vmem((8, 8, CO), F32),
            vmem((2, 27, PITCH, 128), F32),
            vmem((24, CI), F32),
            vmem((8, CI), F32),
            vmem((2, 3, 32, 128), F32),
            vmem((24, CI), F32),
            vmem((8, CI), F32),
            dma((3,)),
            dma((15,)),
            dma((15,)),
            dma((6,)),
            dma((6,)),
            dma((11,)),
            dma((11,)),
            dma((6,)),
            dma((6,)),
            dma((6,)),
            dma((6,)),
            dma((7,)),
            dma((7,)),
            dma((13,)),
            dma((13,)),
        ],
        compiler_params=pltpu.CompilerParams(
            collective_id=0, has_side_effects=True, vmem_limit_bytes=48 * 2**20
        ),
    )(video, kernel, bias_vec.reshape(1, CO), cotangent)
    return activated, video_grad, kernel_grad, bias_grad.reshape(CO)


def solution(mesh):
    return jax.shard_map(
        body,
        mesh=mesh,
        in_specs=(
            P("fsdp", None, "row", "col", None),
            P(None, "fsdp"),
            P(),
            P("fsdp", None, "row", "col", None),
        ),
        out_specs=(
            P("fsdp", None, "row", "col", None),
            P("fsdp", None, "row", "col", None),
            P(("row", "col"), "fsdp"),
            P(),
        ),
        check_vma=False,
    )
```

```python
import math

import jax
import jax.numpy as jnp
from jax import lax
from jax.experimental import pallas as pl
from jax.experimental.pallas import tpu as pltpu
from jax.sharding import PartitionSpec as P

MESH = pl.DeviceIdType.MESH
F32 = jnp.float32
BF16 = jnp.bfloat16

TAPS = 27
CI = 256
CO = 256
SHARD = 64
KROWS = TAPS * CI
TOK = 192
PITCH = 40
VIA_X = 768
ROUND = 4 * VIA_X
SPAN = (KROWS - ROUND) // 2
BLOCK = 864
WINDOW = 224
PIECE = 108
FACTOR = 1.0 / math.sqrt(49152)


def frame_of(t, p):
    return max(t + p - 2, 0)


def nt(a, b):
    return lax.dot_general(a, b, (((1,), (1,)), ((), ())), preferred_element_type=F32)


def nn(a, b):
    return jnp.dot(a, b, preferred_element_type=F32)


def identity(n):
    rows = lax.broadcasted_iota(jnp.int32, (n, n), 0)
    cols = lax.broadcasted_iota(jnp.int32, (n, n), 1)
    return (rows == cols).astype(F32).astype(BF16)


PLANE = 27 * PITCH


def take(flat, start, count, stride):
    return jnp.concatenate(
        [flat[pl.ds(n * PLANE + start, count, stride=stride), :] for n in range(2)], axis=1
    )


def put(flat, start, count, stride, value):
    for n in range(2):
        flat[pl.ds(n * PLANE + start, count, stride=stride), :] = value[:, 128 * n : 128 * n + 128]


def swap_halves(value):
    return jnp.concatenate(
        [pltpu.roll(value[:, 128 * n : 128 * n + 128], 64, 1) for n in range(value.shape[1] // 128)],
        axis=1,
    )


def kernel_body(
    video,
    kernel,
    bias,
    cot,
    act_out,
    vg_out,
    kg_out,
    bg_out,
    kt,
    vid,
    cotv,
    biasv,
    vpad,
    hl_send,
    hc_send,
    hl,
    hu,
    hc,
    patches,
    pt,
    pts,
    dl,
    dlx,
    dls,
    dlsx,
    w,
    ra,
    rb,
    ya,
    xb,
    ys,
    xs,
    sa,
    sb,
    ra2,
    rb2,
    tt,
    zz,
    rz,
    by,
    bx,
    bz,
    g,
    gl_send,
    gc_send,
    gu,
    gl,
    gc,
    lsem,
    k_s,
    k_r,
    h_s,
    h_r,
    c_s,
    c_r,
    r1_s,
    r1_r,
    r2_s,
    r2_r,
    r3_s,
    r3_r,
    b_s,
    b_r,
):
    row = lax.axis_index("row")
    col = lax.axis_index("col")
    y = lax.axis_index("fsdp")
    core = lax.rem(row, 2)
    zl = row // 2
    x = col // 2
    zh = lax.rem(col, 2)
    z = zh * 4 + zl

    def to_y(n):
        return {"row": row, "col": col, "fsdp": lax.rem(y + n, 4)}

    def to_x(n):
        return {"row": row, "col": lax.rem(x + n, 4) * 2 + zh, "fsdp": y}

    def to_z(n):
        there = lax.rem(z + n, 8)
        return {
            "row": lax.rem(there, 4) * 2 + core,
            "col": x * 2 + there // 4,
            "fsdp": y,
        }

    def to_tile(rows, cols):
        return {"row": lax.rem(row + rows + 8, 8), "col": lax.rem(col + cols + 8, 8), "fsdp": y}

    sibling = {"row": row + 1 - 2 * core, "col": col, "fsdp": y}

    def remote(src, dst, ss, rs, where):
        return pltpu.make_async_remote_copy(
            src_ref=src, dst_ref=dst, send_sem=ss, recv_sem=rs, device_id=where, device_id_type=MESH
        )

    partners = [to_y(n) for n in (1, 2, 3)] + [to_x(n) for n in (1, 2, 3)]
    partners += [to_z(n) for n in range(1, 8)] + [sibling]
    partners += [to_tile(a, b) for a, b in ((0, 1), (0, -1), (1, 0), (-1, 0), (1, 1), (-1, -1))]
    barrier = pltpu.get_barrier_semaphore()
    for partner in partners:
        pl.semaphore_signal(barrier, inc=1, device_id=partner, device_id_type=MESH)

    own_rows = pl.multiple_of(y * SHARD, SHARD)
    load_k = pltpu.make_async_copy(kernel, kt.at[pl.ds(own_rows, SHARD), :], lsem.at[0])
    load_v = pltpu.make_async_copy(video.at[0], vid, lsem.at[1])
    load_c = pltpu.make_async_copy(cot.at[0], cotv, lsem.at[2])
    load_b = pltpu.make_async_copy(bias, biasv, lsem.at[3])
    load_k.start()
    load_v.start()
    load_c.start()
    load_b.start()

    pl.semaphore_wait(barrier, len(partners))

    half_rows = pl.multiple_of(y * SHARD + core * 32, 32)
    via = pl.multiple_of(x * VIA_X, 128)

    def shard_rows(n):
        return pl.multiple_of(lax.rem(y + n, 4) * SHARD + core * 32, 32)

    def other_rows(n):
        return pl.multiple_of(lax.rem(y + n, 4) * SHARD + (1 - core) * 32, 32)

    near = pl.ds(core * 32, 32)
    first = []
    for n in (1, 3, 2):
        first.append(
            remote(
                kernel.at[near, pl.ds(via, VIA_X)],
                kt.at[pl.ds(half_rows, 32), pl.ds(via, VIA_X)],
                k_s.at[n - 1],
                k_r.at[n - 1],
                to_y(n),
            )
        )
        first[-1].start()
    direct = []
    for slot, (n, part) in enumerate(((1, 0), (3, 1), (1, 1), (3, 0))):
        lanes = pl.ds(ROUND + part * SPAN, SPAN)
        direct.append(
            remote(
                kernel.at[near, lanes],
                kt.at[pl.ds(half_rows, 32), lanes],
                k_s.at[3 + slot],
                k_r.at[3 + slot],
                to_y(n),
            )
        )
        direct[-1].start()

    load_v.wait()
    for f in range(3):
        for r in range(8):
            for n in range(2):
                vpad[n, (r + 1) * 3 + f, 8:40, :] = vid[f, r, :, 128 * n : 128 * n + 128].astype(F32)
    flat = vpad.reshape(2 * PLANE, 128)
    hl_send[...] = take(flat, 3 * PITCH + 39, 24, PITCH)
    hc_send[0:3, :] = hl_send[21:24, :]

    halos = [
        remote(hl_send, hl, h_s.at[0], h_r.at[0], to_tile(0, 1)),
        remote(vid.at[:, 7], hu, h_s.at[1], h_r.at[1], to_tile(1, 0)),
        remote(hc_send, hc, h_s.at[2], h_r.at[2], to_tile(1, 1)),
    ]
    for copy in halos:
        copy.start()

    passed = []

    def pass_on(n, start, size, slot):
        ref = kt.at[pl.ds(shard_rows(n), 32), pl.ds(start, size)]
        passed.append(remote(ref, ref, c_s.at[slot], c_r.at[slot], sibling))
        passed[-1].start()

    relayed = []
    for at, n in enumerate((1, 3, 2)):
        first[at].wait_recv()
        ref = kt.at[pl.ds(shard_rows(4 - n), 32), pl.ds(via, VIA_X)]
        for m in (1, 3, 2):
            slot = 9 + (n - 1) * 3 + m - 1
            relayed.append(remote(ref, ref, k_s.at[slot], k_r.at[slot], to_x(m)))
            relayed[-1].start()
        pass_on(4 - n, via, VIA_X, 4 + n)

    forward = []
    for slot, (n, part) in enumerate(((1, 0), (3, 1))):
        direct[slot].wait_recv()
        ref = kt.at[pl.ds(shard_rows(4 - n), 32), pl.ds(ROUND + part * SPAN, SPAN)]
        forward.append(remote(ref, ref, k_s.at[7 + slot], k_r.at[7 + slot], to_y(n)))
        forward[-1].start()
        pass_on(4 - n, ROUND + part * SPAN, SPAN, 17 + slot)

    for copy in halos:
        copy.wait_recv()
    for f in range(3):
        top = hu[f].astype(F32)
        top = jnp.where(row > 0, top, 0.0)
        for n in range(2):
            vpad[n, f, 8:40, :] = top[:, 128 * n : 128 * n + 128]
    put(flat, 3 * PITCH + 7, 24, PITCH, jnp.where(col > 0, hl[...], 0.0))
    corner = jnp.where((row > 0) & (col > 0), hc[...], 0.0)
    for f in range(3):
        for n in range(2):
            vpad[n, f, 7:8, :] = corner[f : f + 1, 128 * n : 128 * n + 128]
    for r in range(9):
        for f in range(3):
            for s in range(3):
                block = take(flat, (r * 3 + f) * PITCH + 7 + s, 16, 2).astype(BF16)
                for t in range(3):
                    for p in range(3):
                        if frame_of(t, p) != f:
                            continue
                        for q in range(3):
                            i, odd = divmod(r - q, 2)
                            if odd or not 0 <= i < 4:
                                continue
                            tap = (p * 3 + q) * 3 + s
                            patches[
                                (t * 4 + i) * 16 : (t * 4 + i) * 16 + 16, tap * CI : tap * CI + CI
                            ] = block
    unit = identity(CI)
    for tap in range(TAPS):
        pt[tap * CI : tap * CI + CI, :] = nt(unit, patches[:, tap * CI : tap * CI + CI]).astype(BF16)
    swaps = []
    for n in range(4):
        base = pl.multiple_of(n * 2 * BLOCK + (1 - core) * BLOCK, 32)
        swaps.append(remote(pt.at[pl.ds(base, BLOCK), :], pts.at[n], c_s.at[n], c_r.at[n], sibling))
        swaps[-1].start()

    def pass_relayed(at, n):
        for k, m in enumerate((1, 3, 2)):
            relayed[at * 3 + k].wait_recv()
            from_x = pl.multiple_of(lax.rem(x + 4 - m, 4) * VIA_X, 128)
            pass_on(4 - n, from_x, VIA_X, 8 + (n - 1) * 3 + m - 1)

    pass_relayed(0, 1)
    pass_relayed(1, 3)
    for slot, (n, part) in ((2, (1, 1)), (3, (3, 0))):
        direct[slot].wait_recv()
        pass_on(4 - n, ROUND + part * SPAN, SPAN, 17 + slot)
    pass_relayed(2, 2)
    for part in range(2):
        forward[part].wait_recv()
        pass_on(2, ROUND + part * SPAN, SPAN, 21 + part)
    for copy in passed:
        copy.wait_recv()
    load_k.wait()

    load_b.wait()
    preact = nt(patches[...], kt[...]) + biasv[...]
    sigma = jax.nn.sigmoid(preact)
    act_out[...] = (preact * sigma).astype(BF16).reshape(1, 3, 4, 16, CO)
    load_c.wait()
    slope = cotv[...].reshape(TOK, CO).astype(F32) * sigma * (1.0 + preact * (1.0 - sigma))
    delta = slope.astype(BF16)
    dl[...] = delta
    swap_delta = remote(dl, dls, c_s.at[4], c_r.at[4], sibling)
    swap_delta.start()
    delta_f = delta.astype(F32)
    dlx[...] = swap_halves(delta_f).astype(BF16)
    bias_own = jnp.sum(delta_f, axis=0, keepdims=True)

    g[...] = jnp.zeros_like(g)
    gflat = g.reshape(2 * PLANE, 128)
    for q in range(3):
        for s in range(3):
            d = [
                nn(dl[...], kt[:, ((p * 3 + q) * 3 + s) * CI : ((p * 3 + q) * 3 + s) * CI + CI])
                for p in range(3)
            ]
            frames = [
                d[0][0:64] + d[0][64:128] + d[0][128:192] + d[1][0:64] + d[1][64:128] + d[2][0:64],
                d[1][128:192] + d[2][64:128],
                d[2][128:192],
            ]
            for f in range(3):
                for i in range(4):
                    at = ((q + 2 * i) * 3 + f) * PITCH + 7 + s
                    sofar = take(gflat, at, 16, 2)
                    put(gflat, at, 16, 2, sofar + frames[f][16 * i : 16 * i + 16])
    gl_send[...] = take(gflat, 3 * PITCH + 7, 24, PITCH)
    for f in range(3):
        for n in range(2):
            gc_send[f : f + 1, 128 * n : 128 * n + 128] = g[n, f, 7:8, :]
    edges = [
        remote(gl_send, gl, h_s.at[3], h_r.at[3], to_tile(0, -1)),
        remote(g.at[:, pl.ds(0, 3), pl.ds(8, 32), :], gu, h_s.at[4], h_r.at[4], to_tile(-1, 0)),
        remote(gc_send, gc, h_s.at[5], h_r.at[5], to_tile(-1, -1)),
    ]
    for copy in edges:
        copy.start()

    swap_delta.wait_recv()
    delta_s = dls[...].astype(F32)
    dlsx[...] = swap_halves(delta_s).astype(BF16)
    bias_chip = bias_own + jnp.sum(delta_s, axis=0, keepdims=True)
    by[y] = jnp.broadcast_to(bias_chip, (8, CO))
    for copy in swaps:
        copy.wait_recv()

    low = lax.broadcasted_iota(jnp.int32, (144, 128), 1) < 64
    half = BLOCK // 2

    def weight_rows(part, step):
        lo_at = pl.multiple_of(part * 2 * BLOCK + core * BLOCK + step * 144, 16)
        hi_at = pl.multiple_of((part + 2) * 2 * BLOCK + core * BLOCK + step * 144, 16)
        here = slice(step * 144, step * 144 + 144)
        lo = nn(pt[pl.ds(lo_at, 144), :], dl[...]) + nn(pts[part, here, :], dls[...])
        hi = nn(pt[pl.ds(hi_at, 144), :], dlx[...]) + nn(pts[part + 2, here, :], dlsx[...])
        for n in range(4):
            cols = slice(128 * (n // 2), 128 * (n // 2) + 128)
            if n % 2:
                w[part, n, here, :] = jnp.where(low, hi[:, cols], lo[:, cols]).astype(BF16)
            else:
                w[part, n, here, :] = jnp.where(low, lo[:, cols], hi[:, cols]).astype(BF16)

    def rows_of(part):
        return pl.ds(part * half, half)

    def window(n):
        return pl.ds(pl.multiple_of(16 * (27 * lax.rem(x + n, 4) // 2), 16), WINDOW)

    def lanes_of(part):
        return pl.ds(2 * part, 2)

    turn = ((1, 0), (3, 1))
    bias_y = [remote(by.at[y], by.at[y], b_s.at[n - 1], b_r.at[n - 1], to_y(n)) for n in (1, 2, 3)]
    relay_y, relay_x, plain_y, plain_x, summed_y, summed_x = [], [], [], [], [], []

    for at, (n, part) in enumerate(turn):
        for step in range(3):
            weight_rows(0, 3 * part + step)
        relay_y.append(
            remote(
                w.at[0, lax.rem(y + 2, 4), rows_of(part), :], ya.at[at], r1_s.at[at], r1_r.at[at], to_y(n)
            )
        )
        relay_y[-1].start()
    for copy in bias_y:
        copy.start()
    for at, (n, part) in enumerate(turn):
        rows = rows_of(1 - part)
        plain_y.append(
            remote(
                w.at[0, lax.rem(y + n, 4), rows, :],
                ra.at[at, rows, :],
                r1_s.at[2 + at],
                r1_r.at[2 + at],
                to_y(n),
            )
        )
        plain_y[-1].start()
    for step in range(6):
        weight_rows(1, step)
    for at, (n, part) in enumerate(turn):
        relay_x.append(
            remote(
                w.at[1, lanes_of(part), window(2), :], xb.at[at], r1_s.at[6 + at], r1_r.at[6 + at], to_x(n)
            )
        )
        relay_x[-1].start()
    for at, (n, part) in enumerate(turn):
        lanes = lanes_of(1 - part)
        plain_x.append(
            remote(
                w.at[1, lanes, window(n), :],
                rb.at[at, lanes],
                r1_s.at[8 + at],
                r1_r.at[8 + at],
                to_x(n),
            )
        )
        plain_x[-1].start()
    for at, (n, part) in enumerate(turn):
        relay_y[at].wait_recv()
        rows = rows_of(part)
        own_part = w[0, lax.rem(y + n, 4), rows, :].astype(F32)
        ys[at] = (own_part + ya[at].astype(F32)).astype(BF16)
        summed_y.append(
            remote(ys.at[at], ra.at[at, rows, :], r1_s.at[4 + at], r1_r.at[4 + at], to_y(n))
        )
        summed_y[-1].start()
    for at, (n, part) in enumerate(turn):
        relay_x[at].wait_recv()
        own_part = w[1, lanes_of(part), window(n), :].astype(F32)
        xs[at] = (own_part + xb[at].astype(F32)).astype(BF16)
        summed_x.append(
            remote(xs.at[at], rb.at[at, lanes_of(part)], r1_s.at[10 + at], r1_r.at[10 + at], to_x(n))
        )
        summed_x[-1].start()

    for copy in bias_y:
        copy.wait_recv()
    bx[x] = by[0] + by[1] + by[2] + by[3]
    bias_x = [remote(bx.at[x], bx.at[x], b_s.at[2 + n], b_r.at[2 + n], to_x(n)) for n in (1, 2, 3)]
    for copy in bias_x:
        copy.start()

    for copy in plain_y + summed_y:
        copy.wait_recv()
    sa[...] = (w[0, y].astype(F32) + ra[0].astype(F32) + ra[1].astype(F32)).astype(BF16)
    phase2 = []
    for n in (1, 3, 2):
        start = pl.multiple_of(16 * (27 * lax.rem(x + n, 4) // 2), 16)
        phase2.append(
            remote(sa.at[pl.ds(start, WINDOW), :], ra2.at[n - 1], r2_s.at[n - 1], r2_r.at[n - 1], to_x(n))
        )
        phase2[-1].start()
    own = pl.multiple_of(16 * (27 * x // 2), 16)
    for copy in plain_x + summed_x:
        copy.wait_recv()
    sb[...] = (
        w[1, :, pl.ds(own, WINDOW), :].astype(F32) + rb[0].astype(F32) + rb[1].astype(F32)
    ).astype(BF16)
    for n in (1, 3, 2):
        phase2.append(
            remote(sb.at[lax.rem(y + n, 4)], rb2.at[n - 1], r2_s.at[2 + n], r2_r.at[2 + n], to_y(n))
        )
        phase2[-1].start()

    for copy in edges:
        copy.wait_recv()
    for f in range(3):
        for n in range(2):
            g[n, 24 + f, 8:40, :] += jnp.where(row < 7, gu[n, f], 0.0)
    sofar = take(gflat, 3 * PITCH + 39, 24, PITCH)
    put(gflat, 3 * PITCH + 39, 24, PITCH, sofar + jnp.where(col < 7, gl[...], 0.0))
    corner = jnp.where((row < 7) & (col < 7), gc[...], 0.0)
    for f in range(3):
        for n in range(2):
            g[n, 24 + f, 39:40, :] += corner[f : f + 1, 128 * n : 128 * n + 128]
    for f in range(3):
        for r in range(8):
            for n in range(2):
                vg_out[0, f, r, :, 128 * n : 128 * n + 128] = g[n, (r + 1) * 3 + f, 8:40, :].astype(BF16)


    for copy in bias_x:
        copy.wait_recv()
    bz[z] = bx[0] + bx[1] + bx[2] + bx[3]
    bias_z = [remote(bz.at[z], bz.at[z], b_s.at[5 + n], b_r.at[5 + n], to_z(n)) for n in range(1, 8)]
    for copy in bias_z:
        copy.start()

    odd = lax.rem(y, 2) == 1
    offset = 8 * lax.rem(x, 2)
    first_half = lax.broadcasted_iota(jnp.int32, (64, 128), 1) < 64
    tt[:, WINDOW:, :] = jnp.zeros((2, 24, 128), F32)
    for part in range(2):
        for copy in phase2[3 * part : 3 * part + 3]:
            copy.wait_recv()
        if part == 0:
            total = sa[pl.ds(own, WINDOW), :].astype(F32)
            for n in range(3):
                total = total + ra2[n].astype(F32)
        else:
            total = sb[y].astype(F32)
            for n in range(3):
                total = total + rb2[n].astype(F32)
        tt[part, 0:WINDOW, :] = jnp.where(odd, pltpu.roll(total, 64, 1), total)
        for half in range(2):
            u = tt[part, pl.ds(offset + PIECE * half, 128), :]
            a, b = u[0:64], u[64:128]
            zz[half * 4 + part] = jnp.where(first_half, a, pltpu.roll(b, 64, 1)).astype(BF16)
            zz[half * 4 + 2 + part] = jnp.where(first_half, pltpu.roll(a, 64, 1), b).astype(BF16)
    phase3 = []
    for n in (4, 3, 5, 2, 6, 1, 7):
        phase3.append(
            remote(zz.at[lax.rem(z + n, 8)], rz.at[n - 1], r3_s.at[n - 1], r3_r.at[n - 1], to_z(n))
        )
        phase3[-1].start()

    for copy in bias_z:
        copy.wait_recv()
    total = bz[0]
    for n in range(1, 8):
        total = total + bz[n]
    bg_out[...] = total[0:1] * FACTOR

    for copy in phase3:
        copy.wait_recv()
    total = zz[z].astype(F32)
    for n in range(7):
        total = total + rz[n].astype(F32)
    total = total * FACTOR
    turned = total.T
    kg_out[...] = jnp.concatenate([turned[0:64], turned[64:128]], axis=1)[:, 0:PIECE]

    for copies in (
        first, halos, direct, forward, relayed, swaps, passed, [swap_delta], relay_y, relay_x, plain_y, plain_x,
        summed_y, summed_x, bias_y, edges, bias_x,
        phase2, bias_z, phase3,
    ):
        for copy in copies:
            copy.wait_send()


def write_out(*refs):
    ins, outs, sem = refs[0:4], refs[4:8], refs[8]
    stores = [pltpu.make_async_copy(ins[n], outs[n], sem.at[n]) for n in range(4)]
    for copy in stores:
        copy.start()
    for copy in stores:
        copy.wait()


def body(video, kernel, bias_vec, cotangent):
    dma = pltpu.SemaphoreType.DMA
    vmem = pltpu.VMEM
    shapes = (
        jax.ShapeDtypeStruct((1, 3, 4, 16, CO), BF16),
        jax.ShapeDtypeStruct((1, 3, 8, 32, CI), BF16),
        jax.ShapeDtypeStruct((SHARD, PIECE), F32),
        jax.ShapeDtypeStruct((1, CO), F32),
    )
    operands = [
        pltpu.with_memory_space_constraint(value, pltpu.HBM)
        for value in (video, kernel.T, bias_vec.reshape(1, CO), cotangent)
    ]
    results = pl.pallas_call(
        kernel_body,
        out_shape=shapes,
        in_specs=[
            pl.BlockSpec(memory_space=pl.ANY),
            pl.BlockSpec(memory_space=pl.ANY),
            pl.BlockSpec(memory_space=pl.ANY),
            pl.BlockSpec(memory_space=pl.ANY),
        ],
        out_specs=(pl.BlockSpec(memory_space=pltpu.VMEM),) * 4,
        scratch_shapes=[
            vmem((CO, KROWS), BF16),
            vmem((3, 8, 32, CI), BF16),
            vmem((3, 4, 16, CO), BF16),
            vmem((1, CO), F32),
            vmem((2, 27, PITCH, 128), F32),
            vmem((24, CI), F32),
            vmem((8, CI), F32),
            vmem((24, CI), F32),
            vmem((3, 32, CI), BF16),
            vmem((8, CI), F32),
            vmem((TOK, KROWS), BF16),
            vmem((KROWS, TOK), BF16),
            vmem((4, BLOCK, TOK), BF16),
            vmem((TOK, CO), BF16),
            vmem((TOK, CO), BF16),
            vmem((TOK, CO), BF16),
            vmem((TOK, CO), BF16),
            vmem((2, 4, BLOCK, 128), BF16),
            vmem((2, BLOCK, 128), BF16),
            vmem((2, 4, WINDOW, 128), BF16),
            vmem((2, BLOCK // 2, 128), BF16),
            vmem((2, 2, WINDOW, 128), BF16),
            vmem((2, BLOCK // 2, 128), BF16),
            vmem((2, 2, WINDOW, 128), BF16),
            vmem((BLOCK, 128), BF16),
            vmem((4, WINDOW, 128), BF16),
            vmem((3, WINDOW, 128), BF16),
            vmem((3, WINDOW, 128), BF16),
            vmem((2, WINDOW + 24, 128), F32),
            vmem((8, 64, 128), BF16),
            vmem((7, 64, 128), BF16),
            vmem((4, 8, CO), F32),
            vmem((4, 8, CO), F32),
            vmem((8, 8, CO), F32),
            vmem((2, 27, PITCH, 128), F32),
            vmem((24, CI), F32),
            vmem((8, CI), F32),
            vmem((2, 3, 32, 128), F32),
            vmem((24, CI), F32),
            vmem((8, CI), F32),
            dma((4,)),
            dma((18,)),
            dma((18,)),
            dma((6,)),
            dma((6,)),
            dma((23,)),
            dma((23,)),
            dma((12,)),
            dma((12,)),
            dma((6,)),
            dma((6,)),
            dma((7,)),
            dma((7,)),
            dma((13,)),
            dma((13,)),
        ],
        compiler_params=pltpu.CompilerParams(
            collective_id=0, has_side_effects=True, vmem_limit_bytes=49152 * 2**10
        ),
    )(*operands)
    activated, video_grad, kernel_grad, bias_grad = pl.pallas_call(
        write_out,
        out_shape=shapes,
        in_specs=[pl.BlockSpec(memory_space=pltpu.VMEM)] * 4,
        out_specs=(pl.BlockSpec(memory_space=pl.ANY),) * 4,
        scratch_shapes=[dma((4,))],
        compiler_params=pltpu.CompilerParams(vmem_limit_bytes=4 * 2**20),
    )(*results)
    return activated, video_grad, kernel_grad.T, bias_grad.reshape(CO)


def solution(mesh):
    return jax.shard_map(
        body,
        mesh=mesh,
        in_specs=(
            P("fsdp", None, "row", "col", None),
            P(None, "fsdp"),
            P(),
            P("fsdp", None, "row", "col", None),
        ),
        out_specs=(
            P("fsdp", None, "row", "col", None),
            P("fsdp", None, "row", "col", None),
            P(("row", "col"), "fsdp"),
            P(),
        ),
        check_vma=False,
    )
```

```python
import math

import jax
import jax.numpy as jnp
from jax import lax
from jax.experimental import pallas as pl
from jax.experimental.pallas import tpu as pltpu
from jax.sharding import PartitionSpec as P

MESH = pl.DeviceIdType.MESH
F32 = jnp.float32
BF16 = jnp.bfloat16

TAPS = 27
CI = 256
CO = 256
SHARD = 64
KROWS = TAPS * CI
TOK = 192
PITCH = 40
VIA_X = 768
ROUND = 4 * VIA_X
SPAN = (KROWS - ROUND) // 2
BLOCK = 864
WINDOW = 224
PIECE = 108
FACTOR = 1.0 / math.sqrt(49152)


def frame_of(t, p):
    return max(t + p - 2, 0)


def nt(a, b):
    return lax.dot_general(a, b, (((1,), (1,)), ((), ())), preferred_element_type=F32)


def nn(a, b):
    return jnp.dot(a, b, preferred_element_type=F32)


def identity(n):
    rows = lax.broadcasted_iota(jnp.int32, (n, n), 0)
    cols = lax.broadcasted_iota(jnp.int32, (n, n), 1)
    return (rows == cols).astype(F32).astype(BF16)


PLANE = 27 * PITCH


def take(flat, start, count, stride):
    return jnp.concatenate(
        [flat[pl.ds(n * PLANE + start, count, stride=stride), :] for n in range(2)], axis=1
    )


def put(flat, start, count, stride, value):
    for n in range(2):
        flat[pl.ds(n * PLANE + start, count, stride=stride), :] = value[:, 128 * n : 128 * n + 128]


def swap_halves(value):
    return jnp.concatenate(
        [pltpu.roll(value[:, 128 * n : 128 * n + 128], 64, 1) for n in range(value.shape[1] // 128)],
        axis=1,
    )


def kernel_body(
    video,
    kernel,
    bias,
    cot,
    act_out,
    vg_out,
    kg_out,
    bg_out,
    kt,
    vid,
    cotv,
    biasv,
    vpad,
    hl_send,
    hc_send,
    hl,
    hu,
    hc,
    patches,
    pt,
    pts,
    dl,
    dlx,
    dls,
    dlsx,
    w,
    ra,
    rb,
    ya,
    xb,
    ys,
    xs,
    sa,
    sb,
    ra2,
    rb2,
    tt,
    zz,
    rz,
    by,
    bx,
    bz,
    g,
    gl_send,
    gc_send,
    gu,
    gl,
    gc,
    token,
    lsem,
    k_s,
    k_r,
    h_s,
    h_r,
    c_s,
    c_r,
    r1_s,
    r1_r,
    r2_s,
    r2_r,
    r3_s,
    r3_r,
    b_s,
    b_r,
):
    row = lax.axis_index("row")
    col = lax.axis_index("col")
    y = lax.axis_index("fsdp")
    core = lax.rem(row, 2)
    zl = row // 2
    x = col // 2
    zh = lax.rem(col, 2)
    z = zh * 4 + zl

    def to_y(n):
        return {"row": row, "col": col, "fsdp": lax.rem(y + n, 4)}

    def to_x(n):
        return {"row": row, "col": lax.rem(x + n, 4) * 2 + zh, "fsdp": y}

    def to_z(n):
        there = lax.rem(z + n, 8)
        return {
            "row": lax.rem(there, 4) * 2 + core,
            "col": x * 2 + there // 4,
            "fsdp": y,
        }

    def to_tile(rows, cols):
        return {"row": lax.rem(row + rows + 8, 8), "col": lax.rem(col + cols + 8, 8), "fsdp": y}

    sibling = {"row": row + 1 - 2 * core, "col": col, "fsdp": y}

    def remote(src, dst, ss, rs, where):
        return pltpu.make_async_remote_copy(
            src_ref=src, dst_ref=dst, send_sem=ss, recv_sem=rs, device_id=where, device_id_type=MESH
        )

    partners = [to_y(n) for n in (1, 2, 3)] + [to_x(n) for n in (1, 2, 3)]
    partners += [to_z(1), to_z(7), sibling]
    barrier = pltpu.get_barrier_semaphore()
    for partner in partners:
        pl.semaphore_signal(barrier, inc=1, device_id=partner, device_id_type=MESH)

    own_rows = pl.multiple_of(y * SHARD, SHARD)
    load_k = pltpu.make_async_copy(kernel, kt.at[pl.ds(own_rows, SHARD), :], lsem.at[0])
    load_v = pltpu.make_async_copy(video.at[0], vid, lsem.at[1])
    load_c = pltpu.make_async_copy(cot.at[0], cotv, lsem.at[2])
    load_b = pltpu.make_async_copy(bias, biasv, lsem.at[3])
    load_k.start()
    load_v.start()
    load_c.start()
    load_b.start()

    pl.semaphore_wait(barrier, len(partners))

    half_rows = pl.multiple_of(y * SHARD + core * 32, 32)
    via = pl.multiple_of(x * VIA_X, 128)

    def shard_rows(n):
        return pl.multiple_of(lax.rem(y + n, 4) * SHARD + core * 32, 32)

    def other_rows(n):
        return pl.multiple_of(lax.rem(y + n, 4) * SHARD + (1 - core) * 32, 32)

    near = pl.ds(core * 32, 32)
    first = []
    for n in (1, 3, 2):
        first.append(
            remote(
                kernel.at[near, pl.ds(via, VIA_X)],
                kt.at[pl.ds(half_rows, 32), pl.ds(via, VIA_X)],
                k_s.at[n - 1],
                k_r.at[n - 1],
                to_y(n),
            )
        )
        first[-1].start()
    def tell(step, places):
        for place in places:
            pl.semaphore_signal(token.at[step], inc=1, device_id=place, device_id_type=MESH)

    tell(0, [to_z(1), to_z(7)])
    direct = []
    for slot, (n, part) in enumerate(((1, 0), (3, 1), (1, 1), (3, 0))):
        lanes = pl.ds(ROUND + part * SPAN, SPAN)
        direct.append(
            remote(
                kernel.at[near, lanes],
                kt.at[pl.ds(half_rows, 32), lanes],
                k_s.at[3 + slot],
                k_r.at[3 + slot],
                to_y(n),
            )
        )
        direct[-1].start()

    load_v.wait()
    for f in range(3):
        for r in range(8):
            for n in range(2):
                vpad[n, (r + 1) * 3 + f, 8:40, :] = vid[f, r, :, 128 * n : 128 * n + 128].astype(F32)
    flat = vpad.reshape(2 * PLANE, 128)
    hl_send[...] = take(flat, 3 * PITCH + 39, 24, PITCH)
    hc_send[0:3, :] = hl_send[21:24, :]

    passed = []

    def pass_on(n, start, size, slot):
        ref = kt.at[pl.ds(shard_rows(n), 32), pl.ds(start, size)]
        passed.append(remote(ref, ref, c_s.at[slot], c_r.at[slot], sibling))
        passed[-1].start()

    pl.semaphore_wait(token.at[0], 2)
    tell(1, [to_z(2), to_z(6)])
    relayed = []
    for at, n in enumerate((1, 3, 2)):
        if at == 2:
            pl.semaphore_wait(token.at[1], 2)
            tell(2, [sibling])
        first[at].wait_recv()
        ref = kt.at[pl.ds(shard_rows(4 - n), 32), pl.ds(via, VIA_X)]
        for m in (1, 3, 2):
            slot = 9 + (n - 1) * 3 + m - 1
            relayed.append(remote(ref, ref, k_s.at[slot], k_r.at[slot], to_x(m)))
            relayed[-1].start()
        pass_on(4 - n, via, VIA_X, 4 + n)

    pl.semaphore_wait(token.at[2], 1)
    tell(3, [to_x(1), to_x(3)])
    forward = []
    for slot, (n, part) in enumerate(((1, 0), (3, 1))):
        direct[slot].wait_recv()
        ref = kt.at[pl.ds(shard_rows(4 - n), 32), pl.ds(ROUND + part * SPAN, SPAN)]
        forward.append(remote(ref, ref, k_s.at[7 + slot], k_r.at[7 + slot], to_y(n)))
        forward[-1].start()
        pass_on(4 - n, ROUND + part * SPAN, SPAN, 17 + slot)

    pl.semaphore_wait(token.at[3], 2)
    halos = [
        remote(hl_send, hl, h_s.at[0], h_r.at[0], to_tile(0, 1)),
        remote(vid.at[:, 7], hu, h_s.at[1], h_r.at[1], to_tile(1, 0)),
        remote(hc_send, hc, h_s.at[2], h_r.at[2], to_tile(1, 1)),
    ]
    for copy in halos:
        copy.start()

    def pass_relayed(at, n):
        for k, m in enumerate((1, 3, 2)):
            relayed[at * 3 + k].wait_recv()
            from_x = pl.multiple_of(lax.rem(x + 4 - m, 4) * VIA_X, 128)
            pass_on(4 - n, from_x, VIA_X, 8 + (n - 1) * 3 + m - 1)

    pass_relayed(0, 1)
    pass_relayed(1, 3)
    for slot, (n, part) in ((2, (1, 1)), (3, (3, 0))):
        direct[slot].wait_recv()
        pass_on(4 - n, ROUND + part * SPAN, SPAN, 17 + slot)
    pass_relayed(2, 2)
    for part in range(2):
        forward[part].wait_recv()
        pass_on(2, ROUND + part * SPAN, SPAN, 21 + part)
    for copy in halos:
        copy.wait_recv()
    for f in range(3):
        top = hu[f].astype(F32)
        top = jnp.where(row > 0, top, 0.0)
        for n in range(2):
            vpad[n, f, 8:40, :] = top[:, 128 * n : 128 * n + 128]
    put(flat, 3 * PITCH + 7, 24, PITCH, jnp.where(col > 0, hl[...], 0.0))
    corner = jnp.where((row > 0) & (col > 0), hc[...], 0.0)
    for f in range(3):
        for n in range(2):
            vpad[n, f, 7:8, :] = corner[f : f + 1, 128 * n : 128 * n + 128]
    for r in range(9):
        for f in range(3):
            for s in range(3):
                block = take(flat, (r * 3 + f) * PITCH + 7 + s, 16, 2).astype(BF16)
                for t in range(3):
                    for p in range(3):
                        if frame_of(t, p) != f:
                            continue
                        for q in range(3):
                            i, odd = divmod(r - q, 2)
                            if odd or not 0 <= i < 4:
                                continue
                            tap = (p * 3 + q) * 3 + s
                            patches[
                                (t * 4 + i) * 16 : (t * 4 + i) * 16 + 16, tap * CI : tap * CI + CI
                            ] = block
    unit = identity(CI)
    for tap in range(TAPS):
        pt[tap * CI : tap * CI + CI, :] = nt(unit, patches[:, tap * CI : tap * CI + CI]).astype(BF16)
    swaps = []
    for n in range(4):
        base = pl.multiple_of(n * 2 * BLOCK + (1 - core) * BLOCK, 32)
        swaps.append(remote(pt.at[pl.ds(base, BLOCK), :], pts.at[n], c_s.at[n], c_r.at[n], sibling))
        swaps[-1].start()

    for copy in passed:
        copy.wait_recv()
    load_k.wait()

    load_b.wait()
    preact = nt(patches[...], kt[...]) + biasv[...]
    sigma = jax.nn.sigmoid(preact)
    act_out[...] = (preact * sigma).astype(BF16).reshape(1, 3, 4, 16, CO)
    load_c.wait()
    slope = cotv[...].reshape(TOK, CO).astype(F32) * sigma * (1.0 + preact * (1.0 - sigma))
    delta = slope.astype(BF16)
    dl[...] = delta
    swap_delta = remote(dl, dls, c_s.at[4], c_r.at[4], sibling)
    swap_delta.start()
    delta_f = delta.astype(F32)
    dlx[...] = swap_halves(delta_f).astype(BF16)
    bias_own = jnp.sum(delta_f, axis=0, keepdims=True)

    g[...] = jnp.zeros_like(g)
    gflat = g.reshape(2 * PLANE, 128)
    for q in range(3):
        for s in range(3):
            d = [
                nn(dl[...], kt[:, ((p * 3 + q) * 3 + s) * CI : ((p * 3 + q) * 3 + s) * CI + CI])
                for p in range(3)
            ]
            frames = [
                d[0][0:64] + d[0][64:128] + d[0][128:192] + d[1][0:64] + d[1][64:128] + d[2][0:64],
                d[1][128:192] + d[2][64:128],
                d[2][128:192],
            ]
            for f in range(3):
                for i in range(4):
                    at = ((q + 2 * i) * 3 + f) * PITCH + 7 + s
                    sofar = take(gflat, at, 16, 2)
                    put(gflat, at, 16, 2, sofar + frames[f][16 * i : 16 * i + 16])
    gl_send[...] = take(gflat, 3 * PITCH + 7, 24, PITCH)
    for f in range(3):
        for n in range(2):
            gc_send[f : f + 1, 128 * n : 128 * n + 128] = g[n, f, 7:8, :]
    edges = [
        remote(gl_send, gl, h_s.at[3], h_r.at[3], to_tile(0, -1)),
        remote(g.at[:, pl.ds(0, 3), pl.ds(8, 32), :], gu, h_s.at[4], h_r.at[4], to_tile(-1, 0)),
        remote(gc_send, gc, h_s.at[5], h_r.at[5], to_tile(-1, -1)),
    ]
    for copy in edges:
        copy.start()

    swap_delta.wait_recv()
    delta_s = dls[...].astype(F32)
    dlsx[...] = swap_halves(delta_s).astype(BF16)
    bias_chip = bias_own + jnp.sum(delta_s, axis=0, keepdims=True)
    by[y] = jnp.broadcast_to(bias_chip, (8, CO))
    for copy in swaps:
        copy.wait_recv()

    low = lax.broadcasted_iota(jnp.int32, (144, 128), 1) < 64
    half = BLOCK // 2

    def weight_rows(part, step):
        lo_at = pl.multiple_of(part * 2 * BLOCK + core * BLOCK + step * 144, 16)
        hi_at = pl.multiple_of((part + 2) * 2 * BLOCK + core * BLOCK + step * 144, 16)
        here = slice(step * 144, step * 144 + 144)
        lo = nn(pt[pl.ds(lo_at, 144), :], dl[...]) + nn(pts[part, here, :], dls[...])
        hi = nn(pt[pl.ds(hi_at, 144), :], dlx[...]) + nn(pts[part + 2, here, :], dlsx[...])
        for n in range(4):
            cols = slice(128 * (n // 2), 128 * (n // 2) + 128)
            if n % 2:
                w[part, n, here, :] = jnp.where(low, hi[:, cols], lo[:, cols]).astype(BF16)
            else:
                w[part, n, here, :] = jnp.where(low, lo[:, cols], hi[:, cols]).astype(BF16)

    def rows_of(part):
        return pl.ds(part * half, half)

    def window(n):
        return pl.ds(pl.multiple_of(16 * (27 * lax.rem(x + n, 4) // 2), 16), WINDOW)

    def lanes_of(part):
        return pl.ds(2 * part, 2)

    turn = ((1, 0), (3, 1))
    bias_y = [remote(by.at[y], by.at[y], b_s.at[n - 1], b_r.at[n - 1], to_y(n)) for n in (1, 2, 3)]
    relay_y, relay_x, plain_y, plain_x, summed_y, summed_x = [], [], [], [], [], []

    for at, (n, part) in enumerate(turn):
        for step in range(3):
            weight_rows(0, 3 * part + step)
        relay_y.append(
            remote(
                w.at[0, lax.rem(y + 2, 4), rows_of(part), :], ya.at[at], r1_s.at[at], r1_r.at[at], to_y(n)
            )
        )
        relay_y[-1].start()
    for copy in bias_y:
        copy.start()
    for at, (n, part) in enumerate(turn):
        rows = rows_of(1 - part)
        plain_y.append(
            remote(
                w.at[0, lax.rem(y + n, 4), rows, :],
                ra.at[at, rows, :],
                r1_s.at[2 + at],
                r1_r.at[2 + at],
                to_y(n),
            )
        )
        plain_y[-1].start()
    for step in range(6):
        weight_rows(1, step)
    for at, (n, part) in enumerate(turn):
        relay_x.append(
            remote(
                w.at[1, lanes_of(part), window(2), :], xb.at[at], r1_s.at[6 + at], r1_r.at[6 + at], to_x(n)
            )
        )
        relay_x[-1].start()
    for at, (n, part) in enumerate(turn):
        lanes = lanes_of(1 - part)
        plain_x.append(
            remote(
                w.at[1, lanes, window(n), :],
                rb.at[at, lanes],
                r1_s.at[8 + at],
                r1_r.at[8 + at],
                to_x(n),
            )
        )
        plain_x[-1].start()
    for at, (n, part) in enumerate(turn):
        relay_y[at].wait_recv()
        rows = rows_of(part)
        own_part = w[0, lax.rem(y + n, 4), rows, :].astype(F32)
        ys[at] = (own_part + ya[at].astype(F32)).astype(BF16)
        summed_y.append(
            remote(ys.at[at], ra.at[at, rows, :], r1_s.at[4 + at], r1_r.at[4 + at], to_y(n))
        )
        summed_y[-1].start()
    for at, (n, part) in enumerate(turn):
        relay_x[at].wait_recv()
        own_part = w[1, lanes_of(part), window(n), :].astype(F32)
        xs[at] = (own_part + xb[at].astype(F32)).astype(BF16)
        summed_x.append(
            remote(xs.at[at], rb.at[at, lanes_of(part)], r1_s.at[10 + at], r1_r.at[10 + at], to_x(n))
        )
        summed_x[-1].start()

    for copy in bias_y:
        copy.wait_recv()
    bx[x] = by[0] + by[1] + by[2] + by[3]
    bias_x = [remote(bx.at[x], bx.at[x], b_s.at[2 + n], b_r.at[2 + n], to_x(n)) for n in (1, 2, 3)]
    for copy in bias_x:
        copy.start()

    for copy in plain_y + summed_y:
        copy.wait_recv()
    sa[...] = (w[0, y].astype(F32) + ra[0].astype(F32) + ra[1].astype(F32)).astype(BF16)
    phase2 = []
    for n in (1, 3, 2):
        start = pl.multiple_of(16 * (27 * lax.rem(x + n, 4) // 2), 16)
        phase2.append(
            remote(sa.at[pl.ds(start, WINDOW), :], ra2.at[n - 1], r2_s.at[n - 1], r2_r.at[n - 1], to_x(n))
        )
        phase2[-1].start()
    own = pl.multiple_of(16 * (27 * x // 2), 16)
    for copy in plain_x + summed_x:
        copy.wait_recv()
    sb[...] = (
        w[1, :, pl.ds(own, WINDOW), :].astype(F32) + rb[0].astype(F32) + rb[1].astype(F32)
    ).astype(BF16)
    for n in (1, 3, 2):
        phase2.append(
            remote(sb.at[lax.rem(y + n, 4)], rb2.at[n - 1], r2_s.at[2 + n], r2_r.at[2 + n], to_y(n))
        )
        phase2[-1].start()

    for copy in edges:
        copy.wait_recv()
    for f in range(3):
        for n in range(2):
            g[n, 24 + f, 8:40, :] += jnp.where(row < 7, gu[n, f], 0.0)
    sofar = take(gflat, 3 * PITCH + 39, 24, PITCH)
    put(gflat, 3 * PITCH + 39, 24, PITCH, sofar + jnp.where(col < 7, gl[...], 0.0))
    corner = jnp.where((row < 7) & (col < 7), gc[...], 0.0)
    for f in range(3):
        for n in range(2):
            g[n, 24 + f, 39:40, :] += corner[f : f + 1, 128 * n : 128 * n + 128]
    for f in range(3):
        for r in range(8):
            for n in range(2):
                vg_out[0, f, r, :, 128 * n : 128 * n + 128] = g[n, (r + 1) * 3 + f, 8:40, :].astype(BF16)


    for copy in bias_x:
        copy.wait_recv()
    bz[z] = bx[0] + bx[1] + bx[2] + bx[3]
    bias_z = [remote(bz.at[z], bz.at[z], b_s.at[5 + n], b_r.at[5 + n], to_z(n)) for n in range(1, 8)]
    for copy in bias_z:
        copy.start()

    odd = lax.rem(y, 2) == 1
    offset = 8 * lax.rem(x, 2)
    first_half = lax.broadcasted_iota(jnp.int32, (64, 128), 1) < 64
    tt[:, WINDOW:, :] = jnp.zeros((2, 24, 128), F32)
    for part in range(2):
        for copy in phase2[3 * part : 3 * part + 3]:
            copy.wait_recv()
        if part == 0:
            total = sa[pl.ds(own, WINDOW), :].astype(F32)
            for n in range(3):
                total = total + ra2[n].astype(F32)
        else:
            total = sb[y].astype(F32)
            for n in range(3):
                total = total + rb2[n].astype(F32)
        tt[part, 0:WINDOW, :] = jnp.where(odd, pltpu.roll(total, 64, 1), total)
        for half in range(2):
            u = tt[part, pl.ds(offset + PIECE * half, 128), :]
            a, b = u[0:64], u[64:128]
            zz[half * 4 + part] = jnp.where(first_half, a, pltpu.roll(b, 64, 1)).astype(BF16)
            zz[half * 4 + 2 + part] = jnp.where(first_half, pltpu.roll(a, 64, 1), b).astype(BF16)
    phase3 = []
    for n in (4, 3, 5, 2, 6, 1, 7):
        phase3.append(
            remote(zz.at[lax.rem(z + n, 8)], rz.at[n - 1], r3_s.at[n - 1], r3_r.at[n - 1], to_z(n))
        )
        phase3[-1].start()

    for copy in bias_z:
        copy.wait_recv()
    total = bz[0]
    for n in range(1, 8):
        total = total + bz[n]
    bg_out[...] = total[0:1] * FACTOR

    for copy in phase3:
        copy.wait_recv()
    total = zz[z].astype(F32)
    for n in range(7):
        total = total + rz[n].astype(F32)
    total = total * FACTOR
    turned = total.T
    kg_out[...] = jnp.concatenate([turned[0:64], turned[64:128]], axis=1)[:, 0:PIECE]

    for copies in (
        first, halos, direct, forward, relayed, swaps, passed, [swap_delta], relay_y, relay_x, plain_y, plain_x,
        summed_y, summed_x, bias_y, edges, bias_x,
        phase2, bias_z, phase3,
    ):
        for copy in copies:
            copy.wait_send()


def write_out(*refs):
    ins, outs, sem = refs[0:4], refs[4:8], refs[8]
    stores = [pltpu.make_async_copy(ins[n], outs[n], sem.at[n]) for n in range(4)]
    for copy in stores:
        copy.start()
    for copy in stores:
        copy.wait()


def body(video, kernel, bias_vec, cotangent):
    dma = pltpu.SemaphoreType.DMA
    vmem = pltpu.VMEM
    shapes = (
        jax.ShapeDtypeStruct((1, 3, 4, 16, CO), BF16),
        jax.ShapeDtypeStruct((1, 3, 8, 32, CI), BF16),
        jax.ShapeDtypeStruct((SHARD, PIECE), F32),
        jax.ShapeDtypeStruct((1, CO), F32),
    )
    operands = [
        pltpu.with_memory_space_constraint(value, pltpu.HBM)
        for value in (video, kernel.T, bias_vec.reshape(1, CO), cotangent)
    ]
    results = pl.pallas_call(
        kernel_body,
        out_shape=shapes,
        in_specs=[
            pl.BlockSpec(memory_space=pl.ANY),
            pl.BlockSpec(memory_space=pl.ANY),
            pl.BlockSpec(memory_space=pl.ANY),
            pl.BlockSpec(memory_space=pl.ANY),
        ],
        out_specs=(pl.BlockSpec(memory_space=pltpu.VMEM),) * 4,
        scratch_shapes=[
            vmem((CO, KROWS), BF16),
            vmem((3, 8, 32, CI), BF16),
            vmem((3, 4, 16, CO), BF16),
            vmem((1, CO), F32),
            vmem((2, 27, PITCH, 128), F32),
            vmem((24, CI), F32),
            vmem((8, CI), F32),
            vmem((24, CI), F32),
            vmem((3, 32, CI), BF16),
            vmem((8, CI), F32),
            vmem((TOK, KROWS), BF16),
            vmem((KROWS, TOK), BF16),
            vmem((4, BLOCK, TOK), BF16),
            vmem((TOK, CO), BF16),
            vmem((TOK, CO), BF16),
            vmem((TOK, CO), BF16),
            vmem((TOK, CO), BF16),
            vmem((2, 4, BLOCK, 128), BF16),
            vmem((2, BLOCK, 128), BF16),
            vmem((2, 4, WINDOW, 128), BF16),
            vmem((2, BLOCK // 2, 128), BF16),
            vmem((2, 2, WINDOW, 128), BF16),
            vmem((2, BLOCK // 2, 128), BF16),
            vmem((2, 2, WINDOW, 128), BF16),
            vmem((BLOCK, 128), BF16),
            vmem((4, WINDOW, 128), BF16),
            vmem((3, WINDOW, 128), BF16),
            vmem((3, WINDOW, 128), BF16),
            vmem((2, WINDOW + 24, 128), F32),
            vmem((8, 64, 128), BF16),
            vmem((7, 64, 128), BF16),
            vmem((4, 8, CO), F32),
            vmem((4, 8, CO), F32),
            vmem((8, 8, CO), F32),
            vmem((2, 27, PITCH, 128), F32),
            vmem((24, CI), F32),
            vmem((8, CI), F32),
            vmem((2, 3, 32, 128), F32),
            vmem((24, CI), F32),
            vmem((8, CI), F32),
            pltpu.SemaphoreType.REGULAR((4,)),
            dma((4,)),
            dma((18,)),
            dma((18,)),
            dma((6,)),
            dma((6,)),
            dma((23,)),
            dma((23,)),
            dma((12,)),
            dma((12,)),
            dma((6,)),
            dma((6,)),
            dma((7,)),
            dma((7,)),
            dma((13,)),
            dma((13,)),
        ],
        compiler_params=pltpu.CompilerParams(
            collective_id=0, has_side_effects=True, vmem_limit_bytes=49152 * 2**10
        ),
    )(*operands)
    activated, video_grad, kernel_grad, bias_grad = pl.pallas_call(
        write_out,
        out_shape=shapes,
        in_specs=[pl.BlockSpec(memory_space=pltpu.VMEM)] * 4,
        out_specs=(pl.BlockSpec(memory_space=pl.ANY),) * 4,
        scratch_shapes=[dma((4,))],
        compiler_params=pltpu.CompilerParams(vmem_limit_bytes=4 * 2**20),
    )(*results)
    return activated, video_grad, kernel_grad.T, bias_grad.reshape(CO)


def solution(mesh):
    return jax.shard_map(
        body,
        mesh=mesh,
        in_specs=(
            P("fsdp", None, "row", "col", None),
            P(None, "fsdp"),
            P(),
            P("fsdp", None, "row", "col", None),
        ),
        out_specs=(
            P("fsdp", None, "row", "col", None),
            P("fsdp", None, "row", "col", None),
            P(("row", "col"), "fsdp"),
            P(),
        ),
        check_vma=False,
    )
```
